32 devices in a mesh: tile: 16 (over z, x, core), lev: 2 (over y).
Axes of the slice: x: 2, y: 2, z: 4, core: 2. Of those that a mesh axis runs over, the one named last changes fastest.
Arguments:
- tracers: bfloat16 [8, 8, 256, 128], P(None, 'lev', 'tile'), may hold values from -6 to 6
- wind_field: bfloat16 [3, 8, 256, 128], P(None, 'lev', 'tile'), may hold values from -5 to 5
- regions: int32 [4, 256, 2], P(None, 'tile'), may hold values from 0 to 15, as said below
- stencil_base: int32 [4, 2, 256, 128], P(None, None, 'tile'), may hold values from 0 to 28, as said below
- far_start: int32 [4, 16, 2], replicated, may hold values from 0 to 15, as said below
Outputs:
- tracers_new: bfloat16 [8, 8, 256, 128], P(None, 'lev', 'tile')
- displacement: float32 [3, 8, 256, 128], P(None, 'lev', 'tile')
The draws below stay inside these ranges and needn't reach their ends.
Inputs may be any that keep to these rules, and one draw needn't show every extreme that they name: For an arrival block of band r, regions[k, j, 0] lies in r - 2 to r + 1 and in 0 to 14, and regions[k, j, 1] in 0 to 15. Every column that band r's patches at section k take from band r - 2 lies in the cyclic run of 8 columns from far_start[k, r - 2, 0], and every column taken from band r + 2 in the run from far_start[k, r + 2, 1]. stencil_base[k, 0] is at most 28 and stencil_base[k, 1] at most 12.
All inputs are finite; a program needn't handle non-finite values.
Results may differ from the reference program's by a relative error of at most 0.001.
Values may be sent and summed in bfloat16 or wider, within the bound.
A program may use at most 64 MiB of HBM per device.

```python
import jax
import jax.numpy as jnp
from jax import lax

TRACERS = 8
ITERS = 3
BW = 16
BH = 8
BLOCKS_DEV = 16
BLK = 128
SECTIONS = 4
LEVELS = 8
NBLK = 256
N_TILE = 16


def band_plan(key):
    nblocks = BLOCKS_DEV
    half_run = nblocks // 2
    subkeys = jax.random.split(key, 4)
    shifts = jax.random.randint(subkeys[0], (SECTIONS, N_TILE, 1), 0, nblocks)
    anchor = jax.random.randint(subkeys[1], (SECTIONS, N_TILE, 1), 0, nblocks)
    anchor = anchor.at[0, 0, 0].set((nblocks - 1 - shifts[0, 0, 0]) % nblocks)
    anchor = anchor.at[0, 1, 0].set((nblocks - shifts[0, 1, 0]) % nblocks)
    jet_side = jax.random.randint(subkeys[2], (SECTIONS, N_TILE, 1), 0, 2)
    near_offset = jax.random.randint(subkeys[3], (SECTIONS, N_TILE, nblocks), -1, 1)
    column = jnp.arange(nblocks, dtype=jnp.int32)[None, None, :]
    far_block = (column - anchor) % nblocks < half_run - 1
    offset = jnp.where(far_block, jnp.where(jet_side == 0, -2, 1), near_offset)
    band_ids = jnp.arange(N_TILE, dtype=jnp.int32)[None, :, None]
    upper_band = jnp.clip(band_ids + offset, 0, N_TILE - 2)
    left_col = (column + shifts) % nblocks
    region_table = jnp.stack([upper_band, left_col], axis=-1).reshape(SECTIONS, N_TILE * nblocks, 2)
    run_start = ((anchor + shifts) % nblocks)[:, :, 0]
    toward_high = jnp.roll(run_start, -2, axis=1)
    toward_low = jnp.roll(run_start, 2, axis=1)
    far_table = jnp.stack([toward_high, toward_low], axis=-1)
    return (region_table.astype(jnp.int32), far_table.astype(jnp.int32))


def draw_regions(key, part):
    region_table, far_table = band_plan(jax.random.fold_in(key, 11))
    return region_table


def draw_far_start(key, part):
    region_table, far_table = band_plan(jax.random.fold_in(key, 11))
    return far_table


def draw_stencil_base(key, part):
    subkeys = jax.random.split(jax.random.fold_in(key, 23), 2)
    column_base = jax.random.randint(subkeys[0], (SECTIONS, 1, N_TILE * BLOCKS_DEV, BW * BH), 0, 2 * BW - 3)
    row_base = jax.random.randint(subkeys[1], (SECTIONS, 1, N_TILE * BLOCKS_DEV, BW * BH), 0, 2 * BH - 3)
    return jnp.concatenate([column_base, row_base], axis=1).astype(jnp.int32)


def block_scale(key, extent, pieces, smallest, high):
    def one(axis_at, blocks):
        draws = jax.random.uniform(jax.random.fold_in(jax.random.fold_in(key, 6), axis_at), (blocks,), jnp.float32, smallest / len(pieces), high / len(pieces))
        return jnp.repeat(jnp.exp(draws), extent[axis_at] // blocks).reshape((-1,) + (1,) * (len(extent) - axis_at - 1))

    level = one(*pieces[0])
    for cut in pieces[1:]:
        level = level * one(*cut)
    return level


def centred(own_key, shape, spread, limit, shards=(), held_as=jnp.bfloat16):
    values = spread * jax.random.normal(own_key, shape, jnp.float32)
    if shards:
        values = values * block_scale(own_key, shape, shards, -0.22, 0.18)
    return jnp.clip(values, -limit, limit).astype(held_as)


def setup_inputs(seed: int = 0) -> dict:
    splits = jax.random.split(jax.random.key(seed), 6)
    return {
        "tracers": centred(splits[0], (TRACERS, LEVELS, NBLK, BLK), 1.0, 6.0, ((1, 2), (2, 16))),
        "wind_field": centred(splits[1], (3, LEVELS, NBLK, BLK), 1.0, 5.0, ((1, 2), (2, 16))),
        "regions": draw_regions(jax.random.fold_in(splits[5], 71), 0),
        "stencil_base": draw_stencil_base(jax.random.fold_in(splits[5], 71), 0),
        "far_start": draw_far_start(jax.random.fold_in(splits[5], 71), 0),
    }


def lagrange_cubic(position):
    return [
        -(position - 1.0) * (position - 2.0) * (position - 3.0) / 6.0,
        position * (position - 2.0) * (position - 3.0) / 2.0,
        -position * (position - 1.0) * (position - 3.0) / 2.0,
        position * (position - 1.0) * (position - 2.0) / 6.0,
    ]


def wind_points():
    return [(1, 1), (2, 1), (1, 2), (2, 2)]


def cubic_points():
    listed = []
    for row_step in range(4):
        for column_step in range(4):
            listed.append((column_step, row_step))
    return listed


def patch_index(region_rows, base_rows, own_band, starts, nblocks, points):
    half_run = nblocks // 2
    upper_band = region_rows[:, 0][:, None]
    left_col = region_rows[:, 1][:, None]
    indexes = []
    insides = []
    for column_step, row_step in points:
        column_x = base_rows[0] + column_step
        row_y = base_rows[1] + row_step
        point_band = upper_band + row_y // BH
        point_col = (left_col + column_x // BW) % nblocks
        cell_in = (row_y % BH) * BW + column_x % BW
        offset_band = point_band - own_band
        run_low = (point_col - starts[0]) % nblocks
        run_high = (point_col - starts[1]) % nblocks
        inside = jnp.where(offset_band == -2, run_low < half_run, jnp.where(offset_band == 2, run_high < half_run, True))
        indexes.append(((point_band * nblocks + point_col) * (BW * BH) + cell_in).reshape(-1).astype(jnp.int32))
        insides.append(inside.astype(jnp.float32).reshape(-1))
    return jnp.stack(indexes), jnp.stack(insides)


def reference(tracers, wind_field, regions, stencil_base, far_start):
    n_tracer = tracers.shape[0]
    n_level = tracers.shape[1]
    nblocks = BLOCKS_DEV
    cells_blk = BW * BH
    band_cells = nblocks * cells_blk
    tracer_flat = tracers.reshape(n_tracer, n_level, N_TILE * band_cells)
    wind_flat = wind_field.reshape(3, n_level, N_TILE * band_cells)

    def one_band(own_band):
        first_block = own_band * nblocks
        arrive = lax.dynamic_slice_in_dim(wind_flat, own_band * band_cells, band_cells, 2).astype(jnp.float32)
        displace = jnp.zeros((3, n_level, band_cells), jnp.float32)
        renewed = None
        for section_idx in range(ITERS + 1):
            region_rows = lax.dynamic_slice_in_dim(regions[section_idx], first_block, nblocks, 0)
            base_rows = lax.dynamic_slice_in_dim(stencil_base[section_idx], first_block, nblocks, 1)
            starts = (far_start[section_idx, jnp.maximum(own_band - 2, 0), 0],
                      far_start[section_idx, jnp.minimum(own_band + 2, N_TILE - 1), 1])
            if section_idx < ITERS:
                index_all, inside_all = patch_index(region_rows, base_rows, own_band, starts, nblocks, wind_points())
                gathered = jnp.take(wind_flat, index_all, axis=2, mode="clip")
                frac_x = 0.5 + 0.5 * jnp.tanh(displace[0])
                frac_y = 0.5 + 0.5 * jnp.tanh(displace[1])
                midwind = jnp.zeros((3, n_level, band_cells), jnp.float32)
                for point_idx, (column_step, row_step) in enumerate(wind_points()):
                    weight_x = frac_x if column_step == 2 else 1.0 - frac_x
                    weight_y = frac_y if row_step == 2 else 1.0 - frac_y
                    factor = weight_x * weight_y * inside_all[point_idx]
                    midwind = midwind + factor[None] * gathered[:, :, point_idx].astype(jnp.float32)
                displace = 0.5 * (arrive + midwind)
            else:
                index_all, inside_all = patch_index(region_rows, base_rows, own_band, starts, nblocks, cubic_points())
                gathered = jnp.take(tracer_flat, index_all, axis=2, mode="clip")
                extended = jnp.concatenate([gathered[:, :1], gathered, gathered[:, -1:]], axis=1)
                weight_x = lagrange_cubic(1.5 + 0.5 * jnp.tanh(displace[0]))
                weight_y = lagrange_cubic(1.5 + 0.5 * jnp.tanh(displace[1]))
                factors = []
                for point_idx, (column_step, row_step) in enumerate(cubic_points()):
                    factors.append(weight_x[column_step] * weight_y[row_step] * inside_all[point_idx])
                horizontal = jnp.stack(factors, axis=1)
                vertical = jnp.tanh(displace[2])
                level_weights = [0.5 * vertical * (vertical - 1.0), 1.0 - vertical * vertical, 0.5 * vertical * (vertical + 1.0)]
                summed = jnp.zeros((n_tracer, n_level, band_cells), jnp.float32)
                for level_step in range(3):
                    window = extended[:, level_step:level_step + n_level].astype(jnp.float32)
                    summed = summed + level_weights[level_step][None] * jnp.sum(horizontal[None] * window, axis=2)
                renewed = summed.astype(jnp.bfloat16)
        return renewed, displace

    band_ids = jnp.arange(N_TILE, dtype=jnp.int32)
    renewed, displace = lax.map(one_band, band_ids)
    tracers_new = jnp.transpose(renewed, (1, 2, 0, 3)).reshape(n_tracer, n_level, N_TILE * nblocks, cells_blk)
    displacement = jnp.transpose(displace, (1, 2, 0, 3)).reshape(3, n_level, N_TILE * nblocks, cells_blk)
    return tracers_new, displacement
```

```python
import functools

import jax
import jax.numpy as jnp
from jax import lax
from jax.experimental import pallas as pl
from jax.experimental.pallas import tpu as pltpu
from jax.sharding import PartitionSpec as P

ITERS = 3
BW = 16
BH = 8
MESH = pl.DeviceIdType.MESH


def lagrange_cubic(position):
    return [
        -(position - 1.0) * (position - 2.0) * (position - 3.0) / 6.0,
        position * (position - 2.0) * (position - 3.0) / 2.0,
        -position * (position - 1.0) * (position - 3.0) / 2.0,
        position * (position - 1.0) * (position - 2.0) / 6.0,
    ]


def gather_point(quads, column, row):
    cell = (row & (BH - 1)) * BW + (column & (BW - 1))
    right = column >= BW
    lower = row >= BH
    picked = []
    for parts in zip(*quads):
        g = [jnp.take_along_axis(x, cell, axis=1, mode="promise_in_bounds") for x in parts]
        picked.append(jnp.where(lower, jnp.where(right, g[3], g[2]), jnp.where(right, g[1], g[0])))
    return picked


def kernel(
    n_tile, n_lev, nblocks,
    regions, far_start, base_ref, wind_ref, tracer_ref,
    new_ref, disp_ref,
    wbuf, tbuf, ebuf, pack, edge, edge_pack,
    send_sem, recv_sem,
):
    half = nblocks // 2
    quarter = half // 2
    band = lax.axis_index("tile")
    lev = lax.axis_index("lev")

    def exists(d, e):
        ok = None
        if d < 0:
            ok = band >= -d
        elif d > 0:
            ok = band < n_tile - d
        if e:
            side = lev >= 1 if e < 0 else lev < n_lev - 1
            ok = side if ok is None else jnp.logical_and(ok, side)
        return ok

    partners = [(d, e) for e in (0, -1, 1) for d in (0, -1, 1, -2, 2) if (d, e) != (0, 0)]
    barrier = pltpu.get_barrier_semaphore()
    for d, e in partners:
        @pl.when(exists(d, e))
        def _(d=d, e=e):
            pl.semaphore_signal(barrier, inc=1, device_id=(band + d, lev + e), device_id_type=MESH)

    slot_of = {-2: 0, -1: half, 0: half + nblocks, 1: half + 2 * nblocks, 2: half + 3 * nblocks}

    starts = [far_start[ITERS, band, 0], far_start[ITERS, band, 1]]
    wbuf[2] = wind_ref[...]

    def pack_step(j, carry):
        for side in (0, 1):
            for i in (0, 1):
                block = tracer_ref[lax.rem(starts[side] + 2 * j + i, nblocks)]
                pack[side, 2 * j + i] = block
                wide = block.astype(jnp.float32)
                if i == 0:
                    first = wide
            low = jnp.concatenate([first[0:8], wide[0:8]], axis=0)
            top = jnp.concatenate([first[24:32], wide[24:32]], axis=0)
            edge_pack[0, side, j] = low.astype(jnp.bfloat16)
            edge_pack[1, side, j] = top.astype(jnp.bfloat16)
        return carry

    def edge_step(j, carry):
        first = tracer_ref[2 * j].astype(jnp.float32)
        second = tracer_ref[2 * j + 1].astype(jnp.float32)
        edge[0, j] = jnp.concatenate([first[0:8], second[0:8]], axis=0).astype(jnp.bfloat16)
        edge[1, j] = jnp.concatenate([first[24:32], second[24:32]], axis=0).astype(jnp.bfloat16)
        return carry

    own = slot_of[0]
    tbuf[own : own + nblocks] = tracer_ref[...]
    lax.fori_loop(0, quarter, pack_step, 0)
    lax.fori_loop(0, half, edge_step, 0)

    count = jnp.int32(0)
    for d, e in partners:
        count = count + exists(d, e).astype(jnp.int32)
    pl.semaphore_wait(barrier, count)

    wind_copies, tracer_copies = [], []

    def add(listed, d, e, src, dst):
        at = len(wind_copies) + len(tracer_copies)
        copy = pltpu.make_async_remote_copy(
            src_ref=src, dst_ref=dst, send_sem=send_sem.at[at], recv_sem=recv_sem.at[at],
            device_id=(band + d, lev + e), device_id_type=MESH,
        )
        listed.append((copy, exists(d, e), exists(-d, -e)))

    for d in (-1, 1, -2, 2):
        add(wind_copies, d, 0, wind_ref, wbuf.at[2 - d])
    for d in (-1, 1):
        add(tracer_copies, d, 0, tracer_ref, tbuf.at[pl.ds(slot_of[-d], nblocks)])
    for d in (-2, 2):
        add(tracer_copies, d, 0, pack.at[0 if d > 0 else 1], tbuf.at[pl.ds(slot_of[-d], half)])
    for e in (-1, 1):
        mine = 0 if e < 0 else 1
        theirs = 1 - mine
        for d in (0, -1, 1):
            add(tracer_copies, d, e, edge.at[mine], ebuf.at[theirs, pl.ds(slot_of[-d] // 2, half)])
        for d in (-2, 2):
            add(
                tracer_copies, d, e, edge_pack.at[mine, 0 if d > 0 else 1],
                ebuf.at[theirs, pl.ds(slot_of[-d] // 2, quarter)],
            )
    for copy, sends, _ in wind_copies + tracer_copies:
        @pl.when(sends)
        def _(copy=copy):
            copy.start()

    def drain_recv(copies):
        for copy, _, receives in copies:
            @pl.when(receives)
            def _(copy=copy):
                copy.wait_recv()

    def reads(section, block):
        low = far_start[section, jnp.maximum(band - 2, 0), 0]
        high = far_start[section, jnp.minimum(band + 2, n_tile - 1), 1]
        upper = regions[section, block, 0]
        left = regions[section, block, 1]
        listed = []
        for quad_y in (0, 1):
            for quad_x in (0, 1):
                offset = jnp.clip(upper + quad_y - band, -2, 2)
                col = lax.rem(left + quad_x, nblocks)
                run_low = lax.rem(col - low + nblocks, nblocks)
                run_high = lax.rem(col - high + nblocks, nblocks)
                outside = jnp.logical_or(
                    jnp.logical_and(offset == -2, run_low >= half),
                    jnp.logical_and(offset == 2, run_high >= half),
                )
                inside = jnp.where(outside, 0.0, 1.0).astype(jnp.float32)
                slot = jnp.where(
                    offset == -2,
                    jnp.minimum(run_low, half - 1),
                    jnp.where(
                        offset == 2,
                        half + 3 * nblocks + jnp.minimum(run_high, half - 1),
                        half + (offset + 1) * nblocks + col,
                    ),
                )
                listed.append((offset + 2, col, slot, inside))
        return listed

    def wind_step(block, carry):
        arrive = wind_ref[block].astype(jnp.float32)
        own_parts = [arrive[0:8], arrive[8:16]]
        top_rows = lax.broadcasted_iota(jnp.int32, (8, BW * BH), 0) < 4
        displace = [jnp.zeros((8, BW * BH), jnp.float32)] * 2
        for section in range(ITERS):
            quads = []
            for band_at, col, _, inside in reads(section, block):
                x = wbuf[band_at, col].astype(jnp.float32) * inside
                quads.append([x[0:8], x[8:16]])
            bx = jnp.broadcast_to(base_ref[section, 0, pl.ds(block, 1), :], (8, BW * BH))
            by = jnp.broadcast_to(base_ref[section, 1, pl.ds(block, 1), :], (8, BW * BH))
            frac = 0.5 + 0.5 * jnp.tanh(displace[0])
            turned = jnp.concatenate([frac[4:8], frac[0:4]], axis=0)
            fx = jnp.where(top_rows, frac, turned)
            fy = jnp.where(top_rows, turned, frac)
            total = None
            for b, wy in ((0, 1.0 - fy), (1, fy)):
                for a, wx in ((0, 1.0 - fx), (1, fx)):
                    w = wx * wy
                    got = [w * g for g in gather_point(quads, bx + (1 + a), by + (1 + b))]
                    total = got if total is None else [t + g for t, g in zip(total, got)]
            displace = [0.5 * (o + t) for o, t in zip(own_parts, total)]
        disp_ref[block] = jnp.concatenate(displace, axis=0)
        return carry

    drain_recv(wind_copies)
    lax.fori_loop(0, nblocks, wind_step, 0)
    drain_recv(tracer_copies)

    def tracer_step(block, carry):
        quads = []
        for _, _, slot, inside in reads(ITERS, block):
            x = tbuf[slot].astype(jnp.float32) * inside
            levels = [x[8 * l : 8 * l + 8] for l in range(4)]
            odd = lax.rem(slot, 2) == 1
            pair = lax.div(slot, 2)
            below = ebuf[0, pair].astype(jnp.float32)
            above = ebuf[1, pair].astype(jnp.float32)
            below = jnp.where(lev == 0, levels[0], jnp.where(odd, below[8:16], below[0:8]) * inside)
            above = jnp.where(lev == n_lev - 1, levels[3], jnp.where(odd, above[8:16], above[0:8]) * inside)
            quads.append([below] + levels + [above])
        shape = (8, BW * BH)
        bx = jnp.broadcast_to(base_ref[ITERS, 0, pl.ds(block, 1), :], shape)
        by = jnp.broadcast_to(base_ref[ITERS, 1, pl.ds(block, 1), :], shape)
        bent = jnp.tanh(disp_ref[block])
        lx = lagrange_cubic(1.5 + 0.5 * bent[0:8])
        ly = lagrange_cubic(1.5 + 0.5 * bent[0:8])
        s = bent[8:16]
        up = [0.5 * s * (s - 1.0), 1.0 - s * s, 0.5 * s * (s + 1.0)]

        def row(x, at):
            return jnp.broadcast_to(x[at : at + 1], shape)

        wx = [[row(x, l) for x in lx] for l in range(4)]
        wy = [[row(y, 4 + l) for y in ly] for l in range(4)]
        wv = [[row(v, l) for v in up] for l in range(4)]
        total = [None] * 4
        for n in range(4):
            for m in range(4):
                g = gather_point(quads, bx + m, by + n)
                for l in range(4):
                    h = wv[l][0] * g[l] + wv[l][1] * g[l + 1] + wv[l][2] * g[l + 2]
                    h = h * (wx[l][m] * wy[l][n])
                    total[l] = h if total[l] is None else total[l] + h
        new_ref[block] = jnp.concatenate(total, axis=0).astype(jnp.bfloat16)
        return carry

    lax.fori_loop(0, nblocks, tracer_step, 0)
    for copy, sends, _ in wind_copies + tracer_copies:
        @pl.when(sends)
        def _(copy=copy):
            copy.wait_send()


def body(tracers, wind_field, regions, stencil_base, far_start):
    n_tracer, n_level, nblocks, cells = tracers.shape
    n_tile, n_lev = lax.axis_size("tile"), lax.axis_size("lev")
    wind = jnp.transpose(wind_field.reshape(3 * n_level, nblocks, cells), (1, 0, 2))
    wind = jnp.pad(wind, ((0, 0), (0, 16 - 3 * n_level), (0, 0)))
    tracer = jnp.transpose(tracers, (2, 1, 0, 3)).reshape(nblocks, n_level * n_tracer, cells)
    rows = n_level * n_tracer
    half = nblocks // 2
    vmem = pl.BlockSpec(memory_space=pltpu.VMEM)
    smem = pl.BlockSpec(memory_space=pltpu.SMEM)
    new, disp = pl.pallas_call(
        functools.partial(kernel, n_tile, n_lev, nblocks),
        out_shape=(
            jax.ShapeDtypeStruct((nblocks, rows, cells), jnp.bfloat16),
            jax.ShapeDtypeStruct((nblocks, 16, cells), jnp.float32),
        ),
        in_specs=[smem, smem, vmem, vmem, vmem],
        out_specs=(vmem, vmem),
        scratch_shapes=[
            pltpu.VMEM((5, nblocks, 16, cells), jnp.bfloat16),
            pltpu.VMEM((4 * nblocks, rows, cells), jnp.bfloat16),
            pltpu.VMEM((2, 2 * nblocks, 16, cells), jnp.bfloat16),
            pltpu.VMEM((2, half, rows, cells), jnp.bfloat16),
            pltpu.VMEM((2, half, 16, cells), jnp.bfloat16),
            pltpu.VMEM((2, 2, half // 2, 16, cells), jnp.bfloat16),
            pltpu.SemaphoreType.DMA((18,)),
            pltpu.SemaphoreType.DMA((18,)),
        ],
        compiler_params=pltpu.CompilerParams(
            collective_id=0, has_side_effects=True, vmem_limit_bytes=32 * 1024 * 1024
        ),
    )(regions, far_start, stencil_base, wind, tracer)
    tracers_new = jnp.transpose(new.reshape(nblocks, n_level, n_tracer, cells), (2, 1, 0, 3))
    displacement = jnp.transpose(disp[:, : 3 * n_level], (1, 0, 2)).reshape(3, n_level, nblocks, cells)
    return tracers_new, displacement


def solution(mesh):
    return jax.shard_map(
        body,
        mesh=mesh,
        in_specs=(
            P(None, "lev", "tile", None),
            P(None, "lev", "tile", None),
            P(None, "tile", None),
            P(None, None, "tile", None),
            P(),
        ),
        out_specs=(P(None, "lev", "tile", None), P(None, "lev", "tile", None)),
        check_vma=False,
    )
```

```python
import functools

import jax
import jax.numpy as jnp
from jax import lax
from jax.experimental import pallas as pl
from jax.experimental.pallas import tpu as pltpu
from jax.sharding import PartitionSpec as P

ITERS = 3
BW = 16
BH = 8
MESH = pl.DeviceIdType.MESH


def lagrange_cubic(position):
    return [
        -(position - 1.0) * (position - 2.0) * (position - 3.0) / 6.0,
        position * (position - 2.0) * (position - 3.0) / 2.0,
        -position * (position - 1.0) * (position - 3.0) / 2.0,
        position * (position - 1.0) * (position - 2.0) / 6.0,
    ]


def gather_point(quads, column, row):
    cell = (row & (BH - 1)) * BW + (column & (BW - 1))
    right = column >= BW
    lower = row >= BH
    picked = []
    for parts in zip(*quads):
        g = [jnp.take_along_axis(x, cell, axis=1, mode="promise_in_bounds") for x in parts]
        picked.append(jnp.where(lower, jnp.where(right, g[3], g[2]), jnp.where(right, g[1], g[0])))
    return picked


def kernel(
    n_tile, n_lev, nblocks,
    regions, far_start, base_hbm, wind_ref, tracer_ref,
    new_ref, disp_ref,
    wbuf, tbuf, ebuf, pack, edge, edge_pack, base_ref,
    send_sem, recv_sem, base_sem,
):
    half = nblocks // 2
    quarter = half // 2
    band = lax.axis_index("tile")
    lev = lax.axis_index("lev")

    def exists(d, e):
        ok = None
        if d < 0:
            ok = band >= -d
        elif d > 0:
            ok = band < n_tile - d
        if e:
            side = lev >= 1 if e < 0 else lev < n_lev - 1
            ok = side if ok is None else jnp.logical_and(ok, side)
        return ok

    partners = [(d, e) for e in (0, -1, 1) for d in (0, -1, 1, -2, 2) if (d, e) != (0, 0)]
    barrier = pltpu.get_barrier_semaphore()
    for d, e in partners:
        @pl.when(exists(d, e))
        def _(d=d, e=e):
            pl.semaphore_signal(barrier, inc=1, device_id=(band + d, lev + e), device_id_type=MESH)

    slot_of = {-2: 0, -1: half, 0: half + nblocks, 1: half + 2 * nblocks, 2: half + 3 * nblocks}

    starts = [far_start[ITERS, 0, band], far_start[ITERS, 1, band]]
    wbuf[2] = wind_ref[...]

    def pack_step(j, carry):
        for side in (0, 1):
            for i in (0, 1):
                block = tracer_ref[lax.rem(starts[side] + 2 * j + i, nblocks)]
                pack[side, 2 * j + i] = block
                wide = block.astype(jnp.float32)
                if i == 0:
                    first = wide
            low = jnp.concatenate([first[0:8], wide[0:8]], axis=0)
            top = jnp.concatenate([first[24:32], wide[24:32]], axis=0)
            edge_pack[0, side, j] = low.astype(jnp.bfloat16)
            edge_pack[1, side, j] = top.astype(jnp.bfloat16)
        return carry

    def edge_step(j, carry):
        first = tracer_ref[2 * j].astype(jnp.float32)
        second = tracer_ref[2 * j + 1].astype(jnp.float32)
        edge[0, j] = jnp.concatenate([first[0:8], second[0:8]], axis=0).astype(jnp.bfloat16)
        edge[1, j] = jnp.concatenate([first[24:32], second[24:32]], axis=0).astype(jnp.bfloat16)
        return carry

    own = slot_of[0]
    tbuf[own : own + nblocks] = tracer_ref[...]
    base_copy = pltpu.make_async_copy(base_hbm, base_ref, base_sem)
    base_copy.start()

    count = jnp.int32(0)
    for d, e in partners:
        count = count + exists(d, e).astype(jnp.int32)
    pl.semaphore_wait(barrier, count)

    wind_copies, tracer_copies = [], []

    def add(listed, d, e, src, dst):
        at = len(wind_copies) + len(tracer_copies)
        copy = pltpu.make_async_remote_copy(
            src_ref=src, dst_ref=dst, send_sem=send_sem.at[at], recv_sem=recv_sem.at[at],
            device_id=(band + d, lev + e), device_id_type=MESH,
        )
        listed.append((copy, exists(d, e), exists(-d, -e)))

    for d in (-1, 1, -2, 2):
        add(wind_copies, d, 0, wind_ref, wbuf.at[2 - d])
    for d in (-1, 1):
        add(tracer_copies, d, 0, tracer_ref, tbuf.at[pl.ds(slot_of[-d], nblocks)])
    for d in (-2, 2):
        add(tracer_copies, d, 0, pack.at[0 if d > 0 else 1], tbuf.at[pl.ds(slot_of[-d], half)])
    for e in (-1, 1):
        mine = 0 if e < 0 else 1
        theirs = 1 - mine
        for d in (0, -1, 1):
            add(tracer_copies, d, e, edge.at[mine], ebuf.at[theirs, pl.ds(slot_of[-d] // 2, half)])
        for d in (-2, 2):
            add(
                tracer_copies, d, e, edge_pack.at[mine, 0 if d > 0 else 1],
                ebuf.at[theirs, pl.ds(slot_of[-d] // 2, quarter)],
            )
    def start(copies):
        for copy, sends, _ in copies:
            @pl.when(sends)
            def _(copy=copy):
                copy.start()

    start(wind_copies)
    start(tracer_copies[:2])
    lax.fori_loop(0, quarter, pack_step, 0, unroll=2)
    start(tracer_copies[2:4])
    lax.fori_loop(0, half, edge_step, 0, unroll=2)
    start(tracer_copies[4:])
    base_copy.wait()

    def drain_recv(copies):
        for copy, _, receives in copies:
            @pl.when(receives)
            def _(copy=copy):
                copy.wait_recv()

    def reads(section, block):
        low = far_start[section, 0, jnp.maximum(band - 2, 0)]
        high = far_start[section, 1, jnp.minimum(band + 2, n_tile - 1)]
        upper = regions[section, 0, block]
        left = regions[section, 1, block]
        listed = []
        for quad_y in (0, 1):
            for quad_x in (0, 1):
                offset = jnp.clip(upper + quad_y - band, -2, 2)
                col = lax.rem(left + quad_x, nblocks)
                run_low = lax.rem(col - low + nblocks, nblocks)
                run_high = lax.rem(col - high + nblocks, nblocks)
                outside = jnp.logical_or(
                    jnp.logical_and(offset == -2, run_low >= half),
                    jnp.logical_and(offset == 2, run_high >= half),
                )
                inside = jnp.where(outside, 0.0, 1.0).astype(jnp.float32)
                slot = jnp.where(
                    offset == -2,
                    jnp.minimum(run_low, half - 1),
                    jnp.where(
                        offset == 2,
                        half + 3 * nblocks + jnp.minimum(run_high, half - 1),
                        half + (offset + 1) * nblocks + col,
                    ),
                )
                listed.append((offset + 2, col, slot, inside))
        return listed

    def wind_step(block, carry):
        arrive = wind_ref[block].astype(jnp.float32)
        own_parts = [arrive[0:8], arrive[8:16]]
        top_rows = lax.broadcasted_iota(jnp.int32, (8, BW * BH), 0) < 4
        displace = [jnp.zeros((8, BW * BH), jnp.float32)] * 2
        for section in range(ITERS):
            quads = []
            for band_at, col, _, inside in reads(section, block):
                x = wbuf[band_at, col].astype(jnp.float32) * inside
                quads.append([x[0:8], x[8:16]])
            bx = jnp.broadcast_to(base_ref[section, 0, pl.ds(block, 1), :], (8, BW * BH))
            by = jnp.broadcast_to(base_ref[section, 1, pl.ds(block, 1), :], (8, BW * BH))
            frac = 0.5 + 0.5 * jnp.tanh(displace[0])
            turned = jnp.concatenate([frac[4:8], frac[0:4]], axis=0)
            fx = jnp.where(top_rows, frac, turned)
            fy = jnp.where(top_rows, turned, frac)
            total = None
            for b, wy in ((0, 1.0 - fy), (1, fy)):
                for a, wx in ((0, 1.0 - fx), (1, fx)):
                    w = wx * wy
                    got = [w * g for g in gather_point(quads, bx + (1 + a), by + (1 + b))]
                    total = got if total is None else [t + g for t, g in zip(total, got)]
            displace = [0.5 * (o + t) for o, t in zip(own_parts, total)]
        disp_ref[block] = jnp.concatenate(displace, axis=0)
        return carry

    drain_recv(wind_copies)
    lax.fori_loop(0, nblocks, wind_step, 0, unroll=4)
    drain_recv(tracer_copies)

    def tracer_step(block, carry):
        quads = []
        for _, _, slot, inside in reads(ITERS, block):
            x = tbuf[slot].astype(jnp.float32) * inside
            levels = [x[8 * l : 8 * l + 8] for l in range(4)]
            odd = lax.rem(slot, 2) == 1
            pair = lax.div(slot, 2)
            below = ebuf[0, pair].astype(jnp.float32)
            above = ebuf[1, pair].astype(jnp.float32)
            below = jnp.where(lev == 0, levels[0], jnp.where(odd, below[8:16], below[0:8]) * inside)
            above = jnp.where(lev == n_lev - 1, levels[3], jnp.where(odd, above[8:16], above[0:8]) * inside)
            quads.append([below] + levels + [above])
        shape = (8, BW * BH)
        bx = jnp.broadcast_to(base_ref[ITERS, 0, pl.ds(block, 1), :], shape)
        by = jnp.broadcast_to(base_ref[ITERS, 1, pl.ds(block, 1), :], shape)
        bent = jnp.tanh(disp_ref[block])
        lx = lagrange_cubic(1.5 + 0.5 * bent[0:8])
        ly = lagrange_cubic(1.5 + 0.5 * bent[0:8])
        s = bent[8:16]
        up = [0.5 * s * (s - 1.0), 1.0 - s * s, 0.5 * s * (s + 1.0)]

        def row(x, at):
            return jnp.broadcast_to(x[at : at + 1], shape)

        wx = [[row(x, l) for x in lx] for l in range(4)]
        wy = [[row(y, 4 + l) for y in ly] for l in range(4)]
        wv = [[row(v, l) for v in up] for l in range(4)]
        total = [None] * 4
        for n in range(4):
            for m in range(4):
                g = gather_point(quads, bx + m, by + n)
                for l in range(4):
                    h = wv[l][0] * g[l] + wv[l][1] * g[l + 1] + wv[l][2] * g[l + 2]
                    h = h * (wx[l][m] * wy[l][n])
                    total[l] = h if total[l] is None else total[l] + h
        new_ref[block] = jnp.concatenate(total, axis=0).astype(jnp.bfloat16)
        return carry

    lax.fori_loop(0, nblocks, tracer_step, 0, unroll=2)
    for copy, sends, _ in wind_copies + tracer_copies:
        @pl.when(sends)
        def _(copy=copy):
            copy.wait_send()


def body(tracers, wind_field, regions, stencil_base, far_start):
    n_tracer, n_level, nblocks, cells = tracers.shape
    n_tile, n_lev = lax.axis_size("tile"), lax.axis_size("lev")
    wind = jnp.transpose(wind_field.reshape(3 * n_level, nblocks, cells), (1, 0, 2))
    wind = jnp.pad(wind, ((0, 0), (0, 16 - 3 * n_level), (0, 0)))
    tracer = jnp.transpose(tracers, (2, 1, 0, 3)).reshape(nblocks, n_level * n_tracer, cells)
    rows = n_level * n_tracer
    half = nblocks // 2
    vmem = pl.BlockSpec(memory_space=pltpu.VMEM)
    smem = pl.BlockSpec(memory_space=pltpu.SMEM)
    new, disp = pl.pallas_call(
        functools.partial(kernel, n_tile, n_lev, nblocks),
        out_shape=(
            jax.ShapeDtypeStruct((nblocks, rows, cells), jnp.bfloat16),
            jax.ShapeDtypeStruct((nblocks, 16, cells), jnp.float32),
        ),
        in_specs=[smem, smem, pl.BlockSpec(memory_space=pl.ANY), vmem, vmem],
        out_specs=(vmem, vmem),
        scratch_shapes=[
            pltpu.VMEM((5, nblocks, 16, cells), jnp.bfloat16),
            pltpu.VMEM((4 * nblocks, rows, cells), jnp.bfloat16),
            pltpu.VMEM((2, 2 * nblocks, 16, cells), jnp.bfloat16),
            pltpu.VMEM((2, half, rows, cells), jnp.bfloat16),
            pltpu.VMEM((2, half, 16, cells), jnp.bfloat16),
            pltpu.VMEM((2, 2, half // 2, 16, cells), jnp.bfloat16),
            pltpu.VMEM(stencil_base.shape, jnp.int32),
            pltpu.SemaphoreType.DMA((18,)),
            pltpu.SemaphoreType.DMA((18,)),
            pltpu.SemaphoreType.DMA,
        ],
        compiler_params=pltpu.CompilerParams(
            collective_id=0, has_side_effects=True, vmem_limit_bytes=32 * 1024 * 1024
        ),
    )(jnp.transpose(regions, (0, 2, 1)), jnp.transpose(far_start, (0, 2, 1)), stencil_base, wind, tracer)
    tracers_new = jnp.transpose(new.reshape(nblocks, n_level, n_tracer, cells), (2, 1, 0, 3))
    displacement = jnp.transpose(disp[:, : 3 * n_level], (1, 0, 2)).reshape(3, n_level, nblocks, cells)
    return tracers_new, displacement


def solution(mesh):
    return jax.shard_map(
        body,
        mesh=mesh,
        in_specs=(
            P(None, "lev", "tile", None),
            P(None, "lev", "tile", None),
            P(None, "tile", None),
            P(None, None, "tile", None),
            P(),
        ),
        out_specs=(P(None, "lev", "tile", None), P(None, "lev", "tile", None)),
        check_vma=False,
    )
```

```python
import functools

import jax
import jax.numpy as jnp
from jax import lax
from jax.experimental import pallas as pl
from jax.experimental.pallas import tpu as pltpu
from jax.sharding import PartitionSpec as P

ITERS = 3
BW = 16
BH = 8
MESH = pl.DeviceIdType.MESH


def lagrange_cubic(position):
    return [
        -(position - 1.0) * (position - 2.0) * (position - 3.0) / 6.0,
        position * (position - 2.0) * (position - 3.0) / 2.0,
        -position * (position - 1.0) * (position - 3.0) / 2.0,
        position * (position - 1.0) * (position - 2.0) / 6.0,
    ]


def gather_point(quads, column, row):
    cell = (row & (BH - 1)) * BW + (column & (BW - 1))
    right = column >= BW
    lower = row >= BH
    picked = []
    for parts in zip(*quads):
        g = [jnp.take_along_axis(x, cell, axis=1, mode="promise_in_bounds") for x in parts]
        picked.append(jnp.where(lower, jnp.where(right, g[3], g[2]), jnp.where(right, g[1], g[0])))
    return picked


def kernel(
    n_tile, n_lev, nblocks,
    regions, far_start, base_hbm, wind_ref, tracer_ref,
    new_ref, disp_ref,
    wbuf, tbuf, ebuf, pack, edge, edge_pack, base_ref,
    send_sem, recv_sem, base_sem,
):
    half = nblocks // 2
    quarter = half // 2
    band = lax.axis_index("tile")
    lev = lax.axis_index("lev")

    def exists(d, e):
        ok = None
        if d < 0:
            ok = band >= -d
        elif d > 0:
            ok = band < n_tile - d
        if e:
            side = lev >= 1 if e < 0 else lev < n_lev - 1
            ok = side if ok is None else jnp.logical_and(ok, side)
        return ok

    partners = [(d, e) for e in (0, -1, 1) for d in (0, -1, 1, -2, 2) if (d, e) != (0, 0)]
    barrier = pltpu.get_barrier_semaphore()
    for d, e in partners:
        @pl.when(exists(d, e))
        def _(d=d, e=e):
            pl.semaphore_signal(barrier, inc=1, device_id=(band + d, lev + e), device_id_type=MESH)

    slot_of = {d: (d + 2) * nblocks for d in range(-2, 3)}
    even = lax.rem(band, 2) == 0
    odd = lax.rem(band, 2) == 1

    starts = [far_start[ITERS, 0, band], far_start[ITERS, 1, band]]
    wbuf[2] = wind_ref[...]

    def pack_step(j, carry):
        for side in (0, 1):
            for i in (0, 1):
                block = tracer_ref[lax.rem(starts[side] + 2 * j + i, nblocks)]
                pack[side, 2 * j + i] = block
                wide = block.astype(jnp.float32)
                if i == 0:
                    first = wide
            low = jnp.concatenate([first[0:8], wide[0:8]], axis=0)
            top = jnp.concatenate([first[24:32], wide[24:32]], axis=0)
            edge_pack[0, side, j] = low.astype(jnp.bfloat16)
            edge_pack[1, side, j] = top.astype(jnp.bfloat16)
        return carry

    def edge_step(j, carry):
        first = tracer_ref[2 * j].astype(jnp.float32)
        second = tracer_ref[2 * j + 1].astype(jnp.float32)
        edge[0, j] = jnp.concatenate([first[0:8], second[0:8]], axis=0).astype(jnp.bfloat16)
        edge[1, j] = jnp.concatenate([first[24:32], second[24:32]], axis=0).astype(jnp.bfloat16)
        return carry

    own = slot_of[0]
    tbuf[own : own + nblocks] = tracer_ref[...]
    base_copy = pltpu.make_async_copy(base_hbm, base_ref, base_sem)
    base_copy.start()

    count = jnp.int32(0)
    for d, e in partners:
        count = count + exists(d, e).astype(jnp.int32)
    pl.semaphore_wait(barrier, count)

    wind_copies, tracer_copies = [], []

    def add(listed, d, e, src, dst, sends=None, receives=None):
        at = len(wind_copies) + len(tracer_copies) + len(wind_relays) + len(tracer_relays)
        copy = pltpu.make_async_remote_copy(
            src_ref=src, dst_ref=dst, send_sem=send_sem.at[at], recv_sem=recv_sem.at[at],
            device_id=(band + d, lev + e), device_id_type=MESH,
        )
        if sends is None:
            sends, receives = exists(d, e), exists(-d, -e)
            if abs(d) == 2:
                side = even if d > 0 else odd
                sends, receives = jnp.logical_and(sends, side), jnp.logical_and(receives, side)
        listed.append((copy, sends, receives))

    wind_relays, tracer_relays = [], []

    def relay(listed, buffer, at_of, size, allowed=None):
        for d, mine, to in ((1, even, odd), (-1, odd, even)):
            sends = jnp.logical_and(mine, band >= 1 if d > 0 else band < n_tile - 1)
            receives = jnp.logical_and(to, band >= 2 if d > 0 else band < n_tile - 2)
            if allowed is not None:
                sends, receives = jnp.logical_and(sends, allowed), jnp.logical_and(receives, allowed)
            add(
                listed, d, 0, buffer.at[pl.ds(at_of(-d), size)],
                buffer.at[pl.ds(at_of(-2 * d), size)], sends, receives,
            )

    for d in (-1, 1, -2, 2):
        add(wind_copies, d, 0, wind_ref, wbuf.at[2 - d])
    for d in (-1, 1):
        add(tracer_copies, d, 0, tracer_ref, tbuf.at[pl.ds(slot_of[-d], nblocks)])
    for d in (-2, 2):
        add(tracer_copies, d, 0, pack.at[0 if d > 0 else 1], tbuf.at[pl.ds(slot_of[-d], half)])
    for e in (-1, 1):
        mine = 0 if e < 0 else 1
        theirs = 1 - mine
        for d in (0, -1, 1):
            add(tracer_copies, d, e, edge.at[mine], ebuf.at[theirs, pl.ds(slot_of[-d] // 2, half)])
        for d in (-2, 2):
            add(
                tracer_copies, d, e, edge_pack.at[mine, 0 if d > 0 else 1],
                ebuf.at[theirs, pl.ds(slot_of[-d] // 2, quarter)],
            )
    relay(wind_relays, wbuf, lambda d: d + 2, 1)
    relay(tracer_relays, tbuf, lambda d: slot_of[d], nblocks)
    relay(tracer_relays, ebuf.at[0], lambda d: slot_of[d] // 2, half, lev >= 1)
    relay(tracer_relays, ebuf.at[1], lambda d: slot_of[d] // 2, half, lev < n_lev - 1)

    def start(copies):
        for copy, sends, _ in copies:
            @pl.when(sends)
            def _(copy=copy):
                copy.start()

    start(wind_copies)
    start(tracer_copies[:2])
    lax.fori_loop(0, quarter, pack_step, 0, unroll=2)
    start(tracer_copies[2:4])
    lax.fori_loop(0, half, edge_step, 0, unroll=2)
    start(tracer_copies[4:])
    base_copy.wait()

    def drain_recv(copies):
        for copy, _, receives in copies:
            @pl.when(receives)
            def _(copy=copy):
                copy.wait_recv()

    def reads(section, block):
        low = far_start[section, 0, jnp.maximum(band - 2, 0)]
        high = far_start[section, 1, jnp.minimum(band + 2, n_tile - 1)]
        upper = regions[section, 0, block]
        left = regions[section, 1, block]
        listed = []
        for quad_y in (0, 1):
            for quad_x in (0, 1):
                offset = jnp.clip(upper + quad_y - band, -2, 2)
                col = lax.rem(left + quad_x, nblocks)
                run_low = lax.rem(col - low + nblocks, nblocks)
                run_high = lax.rem(col - high + nblocks, nblocks)
                outside = jnp.logical_or(
                    jnp.logical_and(offset == -2, run_low >= half),
                    jnp.logical_and(offset == 2, run_high >= half),
                )
                inside = jnp.where(outside, 0.0, 1.0).astype(jnp.float32)
                place = jnp.where(
                    jnp.logical_and(offset == -2, even),
                    jnp.minimum(run_low, half - 1),
                    jnp.where(
                        jnp.logical_and(offset == 2, odd), jnp.minimum(run_high, half - 1), col
                    ),
                )
                slot = (offset + 2) * nblocks + place
                listed.append((offset + 2, col, slot, inside))
        return listed

    def wind_step(block, carry):
        arrive = wind_ref[block].astype(jnp.float32)
        own_parts = [arrive[0:8], arrive[8:16]]
        top_rows = lax.broadcasted_iota(jnp.int32, (8, BW * BH), 0) < 4
        displace = [jnp.zeros((8, BW * BH), jnp.float32)] * 2
        for section in range(ITERS):
            quads = []
            for band_at, col, _, inside in reads(section, block):
                x = wbuf[band_at, col].astype(jnp.float32) * inside
                quads.append([x[0:8], x[8:16]])
            bx = jnp.broadcast_to(base_ref[section, 0, pl.ds(block, 1), :], (8, BW * BH))
            by = jnp.broadcast_to(base_ref[section, 1, pl.ds(block, 1), :], (8, BW * BH))
            frac = 0.5 + 0.5 * jnp.tanh(displace[0])
            turned = jnp.concatenate([frac[4:8], frac[0:4]], axis=0)
            fx = jnp.where(top_rows, frac, turned)
            fy = jnp.where(top_rows, turned, frac)
            total = None
            for b, wy in ((0, 1.0 - fy), (1, fy)):
                for a, wx in ((0, 1.0 - fx), (1, fx)):
                    w = wx * wy
                    got = [w * g for g in gather_point(quads, bx + (1 + a), by + (1 + b))]
                    total = got if total is None else [t + g for t, g in zip(total, got)]
            displace = [0.5 * (o + t) for o, t in zip(own_parts, total)]
        disp_ref[block] = jnp.concatenate(displace, axis=0)
        return carry

    drain_recv(wind_copies)
    start(wind_relays)
    drain_recv(wind_relays)
    ahead = 3 * nblocks // 4
    lax.fori_loop(0, ahead, wind_step, 0, unroll=4)
    drain_recv(tracer_copies)
    start(tracer_relays)
    lax.fori_loop(ahead, nblocks, wind_step, 0, unroll=4)
    drain_recv(tracer_relays)

    def tracer_step(block, carry):
        quads = []
        for _, _, slot, inside in reads(ITERS, block):
            x = tbuf[slot].astype(jnp.float32) * inside
            levels = [x[8 * l : 8 * l + 8] for l in range(4)]
            odd = lax.rem(slot, 2) == 1
            pair = lax.div(slot, 2)
            below = ebuf[0, pair].astype(jnp.float32)
            above = ebuf[1, pair].astype(jnp.float32)
            below = jnp.where(lev == 0, levels[0], jnp.where(odd, below[8:16], below[0:8]) * inside)
            above = jnp.where(lev == n_lev - 1, levels[3], jnp.where(odd, above[8:16], above[0:8]) * inside)
            quads.append([below] + levels + [above])
        shape = (8, BW * BH)
        bx = jnp.broadcast_to(base_ref[ITERS, 0, pl.ds(block, 1), :], shape)
        by = jnp.broadcast_to(base_ref[ITERS, 1, pl.ds(block, 1), :], shape)
        bent = jnp.tanh(disp_ref[block])
        lx = lagrange_cubic(1.5 + 0.5 * bent[0:8])
        ly = lagrange_cubic(1.5 + 0.5 * bent[0:8])
        s = bent[8:16]
        up = [0.5 * s * (s - 1.0), 1.0 - s * s, 0.5 * s * (s + 1.0)]

        def row(x, at):
            return jnp.broadcast_to(x[at : at + 1], shape)

        wx = [[row(x, l) for x in lx] for l in range(4)]
        wy = [[row(y, 4 + l) for y in ly] for l in range(4)]
        wv = [[row(v, l) for v in up] for l in range(4)]
        total = [None] * 4
        for n in range(4):
            for m in range(4):
                g = gather_point(quads, bx + m, by + n)
                for l in range(4):
                    h = wv[l][0] * g[l] + wv[l][1] * g[l + 1] + wv[l][2] * g[l + 2]
                    h = h * (wx[l][m] * wy[l][n])
                    total[l] = h if total[l] is None else total[l] + h
        new_ref[block] = jnp.concatenate(total, axis=0).astype(jnp.bfloat16)
        return carry

    lax.fori_loop(0, nblocks, tracer_step, 0, unroll=2)
    for copy, sends, _ in wind_copies + tracer_copies + wind_relays + tracer_relays:
        @pl.when(sends)
        def _(copy=copy):
            copy.wait_send()


def body(tracers, wind_field, regions, stencil_base, far_start):
    n_tracer, n_level, nblocks, cells = tracers.shape
    n_tile, n_lev = lax.axis_size("tile"), lax.axis_size("lev")
    wind = jnp.transpose(wind_field.reshape(3 * n_level, nblocks, cells), (1, 0, 2))
    wind = jnp.pad(wind, ((0, 0), (0, 16 - 3 * n_level), (0, 0)))
    tracer = jnp.transpose(tracers, (2, 1, 0, 3)).reshape(nblocks, n_level * n_tracer, cells)
    rows = n_level * n_tracer
    half = nblocks // 2
    vmem = pl.BlockSpec(memory_space=pltpu.VMEM)
    smem = pl.BlockSpec(memory_space=pltpu.SMEM)
    new, disp = pl.pallas_call(
        functools.partial(kernel, n_tile, n_lev, nblocks),
        out_shape=(
            jax.ShapeDtypeStruct((nblocks, rows, cells), jnp.bfloat16),
            jax.ShapeDtypeStruct((nblocks, 16, cells), jnp.float32),
        ),
        in_specs=[smem, smem, pl.BlockSpec(memory_space=pl.ANY), vmem, vmem],
        out_specs=(vmem, vmem),
        scratch_shapes=[
            pltpu.VMEM((5, nblocks, 16, cells), jnp.bfloat16),
            pltpu.VMEM((5 * nblocks, rows, cells), jnp.bfloat16),
            pltpu.VMEM((2, 5 * half, 16, cells), jnp.bfloat16),
            pltpu.VMEM((2, half, rows, cells), jnp.bfloat16),
            pltpu.VMEM((2, half, 16, cells), jnp.bfloat16),
            pltpu.VMEM((2, 2, half // 2, 16, cells), jnp.bfloat16),
            pltpu.VMEM(stencil_base.shape, jnp.int32),
            pltpu.SemaphoreType.DMA((26,)),
            pltpu.SemaphoreType.DMA((26,)),
            pltpu.SemaphoreType.DMA,
        ],
        compiler_params=pltpu.CompilerParams(
            collective_id=0, has_side_effects=True, vmem_limit_bytes=32 * 1024 * 1024
        ),
    )(jnp.transpose(regions, (0, 2, 1)), jnp.transpose(far_start, (0, 2, 1)), stencil_base, wind, tracer)
    tracers_new = jnp.transpose(new.reshape(nblocks, n_level, n_tracer, cells), (2, 1, 0, 3))
    displacement = jnp.transpose(disp[:, : 3 * n_level], (1, 0, 2)).reshape(3, n_level, nblocks, cells)
    return tracers_new, displacement


def solution(mesh):
    return jax.shard_map(
        body,
        mesh=mesh,
        in_specs=(
            P(None, "lev", "tile", None),
            P(None, "lev", "tile", None),
            P(None, "tile", None),
            P(None, None, "tile", None),
            P(),
        ),
        out_specs=(P(None, "lev", "tile", None), P(None, "lev", "tile", None)),
        check_vma=False,
    )
```

```python
import functools

import jax
import jax.numpy as jnp
from jax import lax
from jax.experimental import pallas as pl
from jax.experimental.pallas import tpu as pltpu
from jax.sharding import PartitionSpec as P

ITERS = 3
BW = 16
BH = 8
MESH = pl.DeviceIdType.MESH


def lagrange_cubic(position):
    return [
        -(position - 1.0) * (position - 2.0) * (position - 3.0) / 6.0,
        position * (position - 2.0) * (position - 3.0) / 2.0,
        -position * (position - 1.0) * (position - 3.0) / 2.0,
        position * (position - 1.0) * (position - 2.0) / 6.0,
    ]


def gather_point(quads, column, row):
    cell = (row & (BH - 1)) * BW + (column & (BW - 1))
    right = column >= BW
    lower = row >= BH
    picked = []
    for parts in zip(*quads):
        g = [jnp.take_along_axis(x, cell, axis=1, mode="promise_in_bounds") for x in parts]
        picked.append(jnp.where(lower, jnp.where(right, g[3], g[2]), jnp.where(right, g[1], g[0])))
    return picked


def kernel(
    n_tile, n_lev, nblocks,
    regions, far_start, base_hbm, wind_ref, tracer_ref,
    new_ref, disp_ref,
    wbuf, tbuf, ebuf, pack, edge, edge_pack, base_ref,
    send_sem, recv_sem, base_sem,
):
    half = nblocks // 2
    quarter = half // 2
    band = lax.axis_index("tile")
    lev = lax.axis_index("lev")

    def exists(d, e):
        ok = None
        if d < 0:
            ok = band >= -d
        elif d > 0:
            ok = band < n_tile - d
        if e:
            side = lev >= 1 if e < 0 else lev < n_lev - 1
            ok = side if ok is None else jnp.logical_and(ok, side)
        return ok

    partners = [(d, e) for e in (0, -1, 1) for d in (0, -1, 1, -2, 2) if (d, e) != (0, 0)]
    barrier = pltpu.get_barrier_semaphore()
    for d, e in partners:
        @pl.when(exists(d, e))
        def _(d=d, e=e):
            pl.semaphore_signal(barrier, inc=1, device_id=(band + d, lev + e), device_id_type=MESH)

    slot_of = {d: (d + 2) * nblocks for d in range(-2, 3)}
    even = lax.rem(band, 2) == 0
    odd = lax.rem(band, 2) == 1

    starts = [far_start[ITERS, 0, band], far_start[ITERS, 1, band]]
    wbuf[2] = wind_ref[...]

    def pack_step(j, carry):
        for side in (0, 1):
            for i in (0, 1):
                block = tracer_ref[lax.rem(starts[side] + 2 * j + i, nblocks)]
                pack[side, 2 * j + i] = block
                wide = block.astype(jnp.float32)
                if i == 0:
                    first = wide
            low = jnp.concatenate([first[0:8], wide[0:8]], axis=0)
            top = jnp.concatenate([first[24:32], wide[24:32]], axis=0)
            edge_pack[0, side, j] = low.astype(jnp.bfloat16)
            edge_pack[1, side, j] = top.astype(jnp.bfloat16)
        return carry

    def edge_step(j, carry):
        first = tracer_ref[2 * j].astype(jnp.float32)
        second = tracer_ref[2 * j + 1].astype(jnp.float32)
        edge[0, j] = jnp.concatenate([first[0:8], second[0:8]], axis=0).astype(jnp.bfloat16)
        edge[1, j] = jnp.concatenate([first[24:32], second[24:32]], axis=0).astype(jnp.bfloat16)
        return carry

    own = slot_of[0]
    tbuf[own : own + nblocks] = tracer_ref[...]
    base_copy = pltpu.make_async_copy(base_hbm, base_ref, base_sem)
    base_copy.start()

    count = jnp.int32(0)
    for d, e in partners:
        count = count + exists(d, e).astype(jnp.int32)
    pl.semaphore_wait(barrier, count)

    wind_copies, tracer_copies = [], []

    def add(listed, d, e, src, dst, sends=None, receives=None):
        at = len(wind_copies) + len(tracer_copies) + len(wind_relays) + len(tracer_relays)
        copy = pltpu.make_async_remote_copy(
            src_ref=src, dst_ref=dst, send_sem=send_sem.at[at], recv_sem=recv_sem.at[at],
            device_id=(band + d, lev + e), device_id_type=MESH,
        )
        if sends is None:
            sends, receives = exists(d, e), exists(-d, -e)
            if abs(d) == 2:
                side = even if d > 0 else odd
                sends, receives = jnp.logical_and(sends, side), jnp.logical_and(receives, side)
        listed.append((copy, sends, receives))

    wind_relays, tracer_relays = [], []

    def relay(listed, buffer, at_of, size, allowed=None):
        for d, mine, to in ((1, even, odd), (-1, odd, even)):
            sends = jnp.logical_and(mine, band >= 1 if d > 0 else band < n_tile - 1)
            receives = jnp.logical_and(to, band >= 2 if d > 0 else band < n_tile - 2)
            if allowed is not None:
                sends, receives = jnp.logical_and(sends, allowed), jnp.logical_and(receives, allowed)
            add(
                listed, d, 0, buffer.at[pl.ds(at_of(-d), size)],
                buffer.at[pl.ds(at_of(-2 * d), size)], sends, receives,
            )

    for d in (-1, 1, -2, 2):
        add(wind_copies, d, 0, wind_ref, wbuf.at[2 - d])
    for d in (-1, 1):
        add(tracer_copies, d, 0, tracer_ref, tbuf.at[pl.ds(slot_of[-d], nblocks)])
    for d in (-2, 2):
        add(tracer_copies, d, 0, pack.at[0 if d > 0 else 1], tbuf.at[pl.ds(slot_of[-d], half)])
    for e in (-1, 1):
        mine = 0 if e < 0 else 1
        theirs = 1 - mine
        for d in (0, -1, 1):
            add(tracer_copies, d, e, edge.at[mine], ebuf.at[theirs, pl.ds(slot_of[-d] // 2, half)])
        for d in (-2, 2):
            add(
                tracer_copies, d, e, edge_pack.at[mine, 0 if d > 0 else 1],
                ebuf.at[theirs, pl.ds(slot_of[-d] // 2, quarter)],
            )
    relay(wind_relays, wbuf, lambda d: d + 2, 1)
    relay(tracer_relays, tbuf, lambda d: slot_of[d], nblocks)
    relay(tracer_relays, ebuf.at[0], lambda d: slot_of[d] // 2, half, lev >= 1)
    relay(tracer_relays, ebuf.at[1], lambda d: slot_of[d] // 2, half, lev < n_lev - 1)

    def start(copies):
        for copy, sends, _ in copies:
            @pl.when(sends)
            def _(copy=copy):
                copy.start()

    start(wind_copies)
    start(tracer_copies[:2])
    lax.fori_loop(0, quarter, pack_step, 0, unroll=2)
    start(tracer_copies[2:4])
    lax.fori_loop(0, half, edge_step, 0, unroll=2)
    start(tracer_copies[4:])
    base_copy.wait()

    def drain_recv(copies):
        for copy, _, receives in copies:
            @pl.when(receives)
            def _(copy=copy):
                copy.wait_recv()

    def reads(section, block):
        low = far_start[section, 0, jnp.maximum(band - 2, 0)]
        high = far_start[section, 1, jnp.minimum(band + 2, n_tile - 1)]
        upper = regions[section, 0, block]
        left = regions[section, 1, block]
        listed = []
        for quad_y in (0, 1):
            for quad_x in (0, 1):
                offset = jnp.clip(upper + quad_y - band, -2, 2)
                col = lax.rem(left + quad_x, nblocks)
                run_low = lax.rem(col - low + nblocks, nblocks)
                run_high = lax.rem(col - high + nblocks, nblocks)
                outside = jnp.logical_or(
                    jnp.logical_and(offset == -2, run_low >= half),
                    jnp.logical_and(offset == 2, run_high >= half),
                )
                inside = jnp.where(outside, 0.0, 1.0).astype(jnp.float32)
                place = jnp.where(
                    jnp.logical_and(offset == -2, even),
                    jnp.minimum(run_low, half - 1),
                    jnp.where(
                        jnp.logical_and(offset == 2, odd), jnp.minimum(run_high, half - 1), col
                    ),
                )
                slot = (offset + 2) * nblocks + place
                listed.append((offset + 2, col, slot, inside))
        return listed

    def wind_step(block, carry):
        arrive = wind_ref[block].astype(jnp.float32)
        own_parts = [arrive[0:8], arrive[8:16]]
        top_rows = lax.broadcasted_iota(jnp.int32, (8, BW * BH), 0) < 4
        displace = [jnp.zeros((8, BW * BH), jnp.float32)] * 2
        for section in range(ITERS):
            quads = []
            for band_at, col, _, inside in reads(section, block):
                x = wbuf[band_at, col].astype(jnp.float32) * inside
                quads.append([x[0:8], x[8:16]])
            bx = jnp.broadcast_to(base_ref[section, 0, pl.ds(block, 1), :], (8, BW * BH))
            by = jnp.broadcast_to(base_ref[section, 1, pl.ds(block, 1), :], (8, BW * BH))
            frac = 0.5 + 0.5 * jnp.tanh(displace[0])
            turned = jnp.concatenate([frac[4:8], frac[0:4]], axis=0)
            fx = jnp.where(top_rows, frac, turned)
            fy = jnp.where(top_rows, turned, frac)
            total = None
            for b, wy in ((0, 1.0 - fy), (1, fy)):
                for a, wx in ((0, 1.0 - fx), (1, fx)):
                    w = wx * wy
                    got = [w * g for g in gather_point(quads, bx + (1 + a), by + (1 + b))]
                    total = got if total is None else [t + g for t, g in zip(total, got)]
            displace = [0.5 * (o + t) for o, t in zip(own_parts, total)]
        disp_ref[block] = jnp.concatenate(displace, axis=0)
        return carry

    drain_recv(wind_copies)
    start(wind_relays)
    drain_recv(wind_relays)
    ahead = 3 * nblocks // 4
    lax.fori_loop(0, ahead, wind_step, 0, unroll=4)
    drain_recv(tracer_copies)
    start(tracer_relays)
    lax.fori_loop(ahead, nblocks, wind_step, 0, unroll=4)
    drain_recv(tracer_relays)

    def tracer_step(block, carry):
        quads = []
        for _, _, slot, inside in reads(ITERS, block):
            x = tbuf[slot].astype(jnp.float32) * inside
            levels = [x[8 * l : 8 * l + 8] for l in range(4)]
            odd = lax.rem(slot, 2) == 1
            pair = lax.div(slot, 2)
            below = ebuf[0, pair].astype(jnp.float32)
            above = ebuf[1, pair].astype(jnp.float32)
            below = jnp.where(lev == 0, levels[0], jnp.where(odd, below[8:16], below[0:8]) * inside)
            above = jnp.where(lev == n_lev - 1, levels[3], jnp.where(odd, above[8:16], above[0:8]) * inside)
            quads.append([below] + levels + [above])
        shape = (8, BW * BH)
        bx = jnp.broadcast_to(base_ref[ITERS, 0, pl.ds(block, 1), :], shape)
        by = jnp.broadcast_to(base_ref[ITERS, 1, pl.ds(block, 1), :], shape)
        bent = jnp.tanh(disp_ref[block])
        lx = lagrange_cubic(1.5 + 0.5 * bent[0:8])
        ly = lagrange_cubic(1.5 + 0.5 * bent[0:8])
        s = bent[8:16]
        up = [0.5 * s * (s - 1.0), 1.0 - s * s, 0.5 * s * (s + 1.0)]

        def row(x, at):
            return jnp.broadcast_to(x[at : at + 1], shape)

        wx = [[row(x, l) for x in lx] for l in range(4)]
        wy = [[row(y, 4 + l) for y in ly] for l in range(4)]
        wv = [[row(v, l) for v in up] for l in range(4)]
        total = [None] * 4
        for n in range(4):
            line = [None] * 4
            for m in range(4):
                g = gather_point(quads, bx + m, by + n)
                for l in range(4):
                    h = wv[l][0] * g[l] + wv[l][1] * g[l + 1] + wv[l][2] * g[l + 2]
                    h = h * wx[l][m]
                    line[l] = h if line[l] is None else line[l] + h
            for l in range(4):
                h = line[l] * wy[l][n]
                total[l] = h if total[l] is None else total[l] + h
        new_ref[block] = jnp.concatenate(total, axis=0).astype(jnp.bfloat16)
        return carry

    lax.fori_loop(0, nblocks, tracer_step, 0, unroll=2)
    for copy, sends, _ in wind_copies + tracer_copies + wind_relays + tracer_relays:
        @pl.when(sends)
        def _(copy=copy):
            copy.wait_send()


def body(tracers, wind_field, regions, stencil_base, far_start):
    n_tracer, n_level, nblocks, cells = tracers.shape
    n_tile, n_lev = lax.axis_size("tile"), lax.axis_size("lev")
    wind = jnp.transpose(wind_field.reshape(3 * n_level, nblocks, cells), (1, 0, 2))
    wind = jnp.pad(wind, ((0, 0), (0, 16 - 3 * n_level), (0, 0)))
    tracer = jnp.transpose(tracers, (2, 1, 0, 3)).reshape(nblocks, n_level * n_tracer, cells)
    rows = n_level * n_tracer
    half = nblocks // 2
    vmem = pl.BlockSpec(memory_space=pltpu.VMEM)
    smem = pl.BlockSpec(memory_space=pltpu.SMEM)
    new, disp = pl.pallas_call(
        functools.partial(kernel, n_tile, n_lev, nblocks),
        out_shape=(
            jax.ShapeDtypeStruct((nblocks, rows, cells), jnp.bfloat16),
            jax.ShapeDtypeStruct((nblocks, 16, cells), jnp.float32),
        ),
        in_specs=[smem, smem, pl.BlockSpec(memory_space=pl.ANY), vmem, vmem],
        out_specs=(vmem, vmem),
        scratch_shapes=[
            pltpu.VMEM((5, nblocks, 16, cells), jnp.bfloat16),
            pltpu.VMEM((5 * nblocks, rows, cells), jnp.bfloat16),
            pltpu.VMEM((2, 5 * half, 16, cells), jnp.bfloat16),
            pltpu.VMEM((2, half, rows, cells), jnp.bfloat16),
            pltpu.VMEM((2, half, 16, cells), jnp.bfloat16),
            pltpu.VMEM((2, 2, half // 2, 16, cells), jnp.bfloat16),
            pltpu.VMEM(stencil_base.shape, jnp.int32),
            pltpu.SemaphoreType.DMA((26,)),
            pltpu.SemaphoreType.DMA((26,)),
            pltpu.SemaphoreType.DMA,
        ],
        compiler_params=pltpu.CompilerParams(
            collective_id=0, has_side_effects=True, vmem_limit_bytes=32 * 1024 * 1024
        ),
    )(jnp.transpose(regions, (0, 2, 1)), jnp.transpose(far_start, (0, 2, 1)), stencil_base, wind, tracer)
    tracers_new = jnp.transpose(new.reshape(nblocks, n_level, n_tracer, cells), (2, 1, 0, 3))
    displacement = jnp.transpose(disp[:, : 3 * n_level], (1, 0, 2)).reshape(3, n_level, nblocks, cells)
    return tracers_new, displacement


def solution(mesh):
    return jax.shard_map(
        body,
        mesh=mesh,
        in_specs=(
            P(None, "lev", "tile", None),
            P(None, "lev", "tile", None),
            P(None, "tile", None),
            P(None, None, "tile", None),
            P(),
        ),
        out_specs=(P(None, "lev", "tile", None), P(None, "lev", "tile", None)),
        check_vma=False,
    )
```

```python
import functools

import jax
import jax.numpy as jnp
from jax import lax
from jax.experimental import pallas as pl
from jax.experimental.pallas import tpu as pltpu
from jax.sharding import PartitionSpec as P

ITERS = 3
BW = 16
BH = 8
MESH = pl.DeviceIdType.MESH


def lagrange_cubic(position):
    return [
        -(position - 1.0) * (position - 2.0) * (position - 3.0) / 6.0,
        position * (position - 2.0) * (position - 3.0) / 2.0,
        -position * (position - 1.0) * (position - 3.0) / 2.0,
        position * (position - 1.0) * (position - 2.0) / 6.0,
    ]


def gather_point(quads, column, row):
    cell = (row & (BH - 1)) * BW + (column & (BW - 1))
    right = column >= BW
    lower = row >= BH
    picked = []
    for parts in zip(*quads):
        g = [jnp.take_along_axis(x, cell, axis=1, mode="promise_in_bounds") for x in parts]
        picked.append(jnp.where(lower, jnp.where(right, g[3], g[2]), jnp.where(right, g[1], g[0])))
    return picked


def kernel(
    n_tile, n_lev, nblocks,
    regions, far_start, base_hbm, wind_ref, tracer_ref,
    new_ref, disp_ref,
    wbuf, tbuf, ebuf, pack, edge, edge_pack, base_ref,
    send_sem, recv_sem, base_sem,
):
    half = nblocks // 2
    quarter = half // 2
    band = lax.axis_index("tile")
    lev = lax.axis_index("lev")

    def exists(d, e):
        ok = None
        if d < 0:
            ok = band >= -d
        elif d > 0:
            ok = band < n_tile - d
        if e:
            side = lev >= 1 if e < 0 else lev < n_lev - 1
            ok = side if ok is None else jnp.logical_and(ok, side)
        return ok

    partners = [(d, e) for e in (0, -1, 1) for d in (0, -1, 1, -2, 2) if (d, e) != (0, 0)]
    barrier = pltpu.get_barrier_semaphore()
    for d, e in partners:
        @pl.when(exists(d, e))
        def _(d=d, e=e):
            pl.semaphore_signal(barrier, inc=1, device_id=(band + d, lev + e), device_id_type=MESH)

    slot_of = {d: (d + 2) * nblocks for d in range(-2, 3)}
    even = lax.rem(band, 2) == 0
    odd = lax.rem(band, 2) == 1

    starts = [far_start[ITERS, 0, band], far_start[ITERS, 1, band]]
    wbuf[2] = wind_ref[...]

    def pack_step(j, carry):
        for side in (0, 1):
            for i in (0, 1):
                block = tracer_ref[lax.rem(starts[side] + 2 * j + i, nblocks)]
                pack[side, 2 * j + i] = block
                wide = block.astype(jnp.float32)
                if i == 0:
                    first = wide
            low = jnp.concatenate([first[0:8], wide[0:8]], axis=0)
            top = jnp.concatenate([first[24:32], wide[24:32]], axis=0)
            edge_pack[0, side, j] = low.astype(jnp.bfloat16)
            edge_pack[1, side, j] = top.astype(jnp.bfloat16)
        return carry

    def edge_step(j, carry):
        first = tracer_ref[2 * j].astype(jnp.float32)
        second = tracer_ref[2 * j + 1].astype(jnp.float32)
        edge[0, j] = jnp.concatenate([first[0:8], second[0:8]], axis=0).astype(jnp.bfloat16)
        edge[1, j] = jnp.concatenate([first[24:32], second[24:32]], axis=0).astype(jnp.bfloat16)
        return carry

    own = slot_of[0]
    tbuf[own : own + nblocks] = tracer_ref[...]
    base_copy = pltpu.make_async_copy(base_hbm, base_ref, base_sem)
    base_copy.start()

    count = jnp.int32(0)
    for d, e in partners:
        count = count + exists(d, e).astype(jnp.int32)
    pl.semaphore_wait(barrier, count)

    wind_copies, tracer_copies = [], []

    def add(listed, d, e, src, dst, sends=None, receives=None):
        at = len(wind_copies) + len(tracer_copies) + len(wind_relays) + len(tracer_relays)
        copy = pltpu.make_async_remote_copy(
            src_ref=src, dst_ref=dst, send_sem=send_sem.at[at], recv_sem=recv_sem.at[at],
            device_id=(band + d, lev + e), device_id_type=MESH,
        )
        if sends is None:
            sends, receives = exists(d, e), exists(-d, -e)
            if abs(d) == 2:
                side = even if d > 0 else odd
                sends, receives = jnp.logical_and(sends, side), jnp.logical_and(receives, side)
        listed.append((copy, sends, receives))

    wind_relays, tracer_relays = [], []

    def relay(listed, buffer, at_of, size, allowed=None):
        for d, mine, to in ((1, even, odd), (-1, odd, even)):
            sends = jnp.logical_and(mine, band >= 1 if d > 0 else band < n_tile - 1)
            receives = jnp.logical_and(to, band >= 2 if d > 0 else band < n_tile - 2)
            if allowed is not None:
                sends, receives = jnp.logical_and(sends, allowed), jnp.logical_and(receives, allowed)
            add(
                listed, d, 0, buffer.at[pl.ds(at_of(-d), size)],
                buffer.at[pl.ds(at_of(-2 * d), size)], sends, receives,
            )

    for d in (-1, 1, -2, 2):
        add(wind_copies, d, 0, wind_ref, wbuf.at[2 - d])
    for d in (-1, 1):
        add(tracer_copies, d, 0, tracer_ref, tbuf.at[pl.ds(slot_of[-d], nblocks)])
    for d in (-2, 2):
        add(tracer_copies, d, 0, pack.at[0 if d > 0 else 1], tbuf.at[pl.ds(slot_of[-d], half)])
    for e in (-1, 1):
        mine = 0 if e < 0 else 1
        theirs = 1 - mine
        for d in (0, -1, 1):
            add(tracer_copies, d, e, edge.at[mine], ebuf.at[theirs, pl.ds(slot_of[-d] // 2, half)])
        for d in (-2, 2):
            add(
                tracer_copies, d, e, edge_pack.at[mine, 0 if d > 0 else 1],
                ebuf.at[theirs, pl.ds(slot_of[-d] // 2, quarter)],
            )
    relay(wind_relays, wbuf, lambda d: d + 2, 1)
    relay(tracer_relays, tbuf, lambda d: slot_of[d], nblocks)
    relay(tracer_relays, ebuf.at[0], lambda d: slot_of[d] // 2, half, lev >= 1)
    relay(tracer_relays, ebuf.at[1], lambda d: slot_of[d] // 2, half, lev < n_lev - 1)

    def start(copies):
        for copy, sends, _ in copies:
            @pl.when(sends)
            def _(copy=copy):
                copy.start()

    start(wind_copies)
    start(tracer_copies[:2])
    lax.fori_loop(0, quarter, pack_step, 0, unroll=2)
    start(tracer_copies[2:4])
    lax.fori_loop(0, half, edge_step, 0, unroll=2)
    start(tracer_copies[4:])
    base_copy.wait()

    def drain_recv(copies):
        for copy, _, receives in copies:
            @pl.when(receives)
            def _(copy=copy):
                copy.wait_recv()

    def reads(section, block):
        low = far_start[section, 0, jnp.maximum(band - 2, 0)]
        high = far_start[section, 1, jnp.minimum(band + 2, n_tile - 1)]
        upper = regions[section, 0, block]
        left = regions[section, 1, block]
        listed = []
        for quad_y in (0, 1):
            for quad_x in (0, 1):
                offset = jnp.clip(upper + quad_y - band, -2, 2)
                col = lax.rem(left + quad_x, nblocks)
                run_low = lax.rem(col - low + nblocks, nblocks)
                run_high = lax.rem(col - high + nblocks, nblocks)
                outside = jnp.logical_or(
                    jnp.logical_and(offset == -2, run_low >= half),
                    jnp.logical_and(offset == 2, run_high >= half),
                )
                inside = jnp.where(outside, 0.0, 1.0).astype(jnp.float32)
                place = jnp.where(
                    jnp.logical_and(offset == -2, even),
                    jnp.minimum(run_low, half - 1),
                    jnp.where(
                        jnp.logical_and(offset == 2, odd), jnp.minimum(run_high, half - 1), col
                    ),
                )
                slot = (offset + 2) * nblocks + place
                listed.append((offset + 2, col, slot, inside))
        return listed

    def wind_step(block, carry):
        arrive = wind_ref[block].astype(jnp.float32)
        own_parts = [arrive[0:8], arrive[8:16]]
        top_rows = lax.broadcasted_iota(jnp.int32, (8, BW * BH), 0) < 4
        displace = [jnp.zeros((8, BW * BH), jnp.float32)] * 2
        for section in range(ITERS):
            quads = []
            for band_at, col, _, inside in reads(section, block):
                x = wbuf[band_at, col].astype(jnp.float32) * inside
                quads.append([x[0:8], x[8:16]])
            bx = jnp.broadcast_to(base_ref[section, 0, pl.ds(block, 1), :], (8, BW * BH))
            by = jnp.broadcast_to(base_ref[section, 1, pl.ds(block, 1), :], (8, BW * BH))
            frac = 0.5 + 0.5 * jnp.tanh(displace[0])
            turned = jnp.concatenate([frac[4:8], frac[0:4]], axis=0)
            fx = jnp.where(top_rows, frac, turned)
            fy = jnp.where(top_rows, turned, frac)
            total = None
            for b, wy in ((0, 1.0 - fy), (1, fy)):
                for a, wx in ((0, 1.0 - fx), (1, fx)):
                    w = wx * wy
                    got = [w * g for g in gather_point(quads, bx + (1 + a), by + (1 + b))]
                    total = got if total is None else [t + g for t, g in zip(total, got)]
            displace = [0.5 * (o + t) for o, t in zip(own_parts, total)]
        disp_ref[block] = jnp.concatenate(displace, axis=0)
        return carry

    drain_recv(wind_copies)
    start(wind_relays)
    drain_recv(wind_relays)
    ahead = 3 * nblocks // 4
    lax.fori_loop(0, ahead, wind_step, 0, unroll=4)
    drain_recv(tracer_copies[:2])
    start(tracer_relays[:2])
    drain_recv(tracer_copies[2:])
    start(tracer_relays[2:])
    lax.fori_loop(ahead, nblocks, wind_step, 0, unroll=4)
    drain_recv(tracer_relays)

    def tracer_step(block, carry):
        quads = []
        for _, _, slot, inside in reads(ITERS, block):
            x = tbuf[slot].astype(jnp.float32) * inside
            levels = [x[8 * l : 8 * l + 8] for l in range(4)]
            odd = lax.rem(slot, 2) == 1
            pair = lax.div(slot, 2)
            below = ebuf[0, pair].astype(jnp.float32)
            above = ebuf[1, pair].astype(jnp.float32)
            below = jnp.where(lev == 0, levels[0], jnp.where(odd, below[8:16], below[0:8]) * inside)
            above = jnp.where(lev == n_lev - 1, levels[3], jnp.where(odd, above[8:16], above[0:8]) * inside)
            quads.append([below] + levels + [above])
        shape = (8, BW * BH)
        bx = jnp.broadcast_to(base_ref[ITERS, 0, pl.ds(block, 1), :], shape)
        by = jnp.broadcast_to(base_ref[ITERS, 1, pl.ds(block, 1), :], shape)
        bent = jnp.tanh(disp_ref[block])
        lx = lagrange_cubic(1.5 + 0.5 * bent[0:8])
        ly = lagrange_cubic(1.5 + 0.5 * bent[0:8])
        s = bent[8:16]
        up = [0.5 * s * (s - 1.0), 1.0 - s * s, 0.5 * s * (s + 1.0)]

        def row(x, at):
            return jnp.broadcast_to(x[at : at + 1], shape)

        wx = [[row(x, l) for x in lx] for l in range(4)]
        wy = [[row(y, 4 + l) for y in ly] for l in range(4)]
        wv = [[row(v, l) for v in up] for l in range(4)]
        total = [None] * 4
        for n in range(4):
            for m in range(4):
                g = gather_point(quads, bx + m, by + n)
                for l in range(4):
                    h = wv[l][0] * g[l] + wv[l][1] * g[l + 1] + wv[l][2] * g[l + 2]
                    h = h * (wx[l][m] * wy[l][n])
                    total[l] = h if total[l] is None else total[l] + h
        new_ref[block] = jnp.concatenate(total, axis=0).astype(jnp.bfloat16)
        return carry

    lax.fori_loop(0, nblocks, tracer_step, 0, unroll=2)
    for copy, sends, _ in wind_copies + tracer_copies + wind_relays + tracer_relays:
        @pl.when(sends)
        def _(copy=copy):
            copy.wait_send()


def body(tracers, wind_field, regions, stencil_base, far_start):
    n_tracer, n_level, nblocks, cells = tracers.shape
    n_tile, n_lev = lax.axis_size("tile"), lax.axis_size("lev")
    wind = jnp.transpose(wind_field.reshape(3 * n_level, nblocks, cells), (1, 0, 2))
    wind = jnp.pad(wind, ((0, 0), (0, 16 - 3 * n_level), (0, 0)))
    tracer = jnp.transpose(tracers, (2, 1, 0, 3)).reshape(nblocks, n_level * n_tracer, cells)
    rows = n_level * n_tracer
    half = nblocks // 2
    vmem = pl.BlockSpec(memory_space=pltpu.VMEM)
    smem = pl.BlockSpec(memory_space=pltpu.SMEM)
    new, disp = pl.pallas_call(
        functools.partial(kernel, n_tile, n_lev, nblocks),
        out_shape=(
            jax.ShapeDtypeStruct((nblocks, rows, cells), jnp.bfloat16),
            jax.ShapeDtypeStruct((nblocks, 16, cells), jnp.float32),
        ),
        in_specs=[smem, smem, pl.BlockSpec(memory_space=pl.ANY), vmem, vmem],
        out_specs=(vmem, vmem),
        scratch_shapes=[
            pltpu.VMEM((5, nblocks, 16, cells), jnp.bfloat16),
            pltpu.VMEM((5 * nblocks, rows, cells), jnp.bfloat16),
            pltpu.VMEM((2, 5 * half, 16, cells), jnp.bfloat16),
            pltpu.VMEM((2, half, rows, cells), jnp.bfloat16),
            pltpu.VMEM((2, half, 16, cells), jnp.bfloat16),
            pltpu.VMEM((2, 2, half // 2, 16, cells), jnp.bfloat16),
            pltpu.VMEM(stencil_base.shape, jnp.int32),
            pltpu.SemaphoreType.DMA((26,)),
            pltpu.SemaphoreType.DMA((26,)),
            pltpu.SemaphoreType.DMA,
        ],
        compiler_params=pltpu.CompilerParams(
            collective_id=0, has_side_effects=True, vmem_limit_bytes=32 * 1024 * 1024
        ),
    )(jnp.transpose(regions, (0, 2, 1)), jnp.transpose(far_start, (0, 2, 1)), stencil_base, wind, tracer)
    tracers_new = jnp.transpose(new.reshape(nblocks, n_level, n_tracer, cells), (2, 1, 0, 3))
    displacement = jnp.transpose(disp[:, : 3 * n_level], (1, 0, 2)).reshape(3, n_level, nblocks, cells)
    return tracers_new, displacement


def solution(mesh):
    return jax.shard_map(
        body,
        mesh=mesh,
        in_specs=(
            P(None, "lev", "tile", None),
            P(None, "lev", "tile", None),
            P(None, "tile", None),
            P(None, None, "tile", None),
            P(),
        ),
        out_specs=(P(None, "lev", "tile", None), P(None, "lev", "tile", None)),
        check_vma=False,
    )
```
